32 devices in a mesh: section: 4 (over y, x), expert: 8 (over z, core).
Axes of the slice: x: 2, y: 2, z: 4, core: 2. Of those that a mesh axis runs over, the one named last changes fastest.
Arguments:
- tokens: bfloat16 [6, 192, 1440], P(None, 'expert'), may hold values from -36 to 36
- norm_gain: float32 [4, 1440], P('section'), may hold values from 0.5 to 1.5
- gate_up: bfloat16 [4, 8, 1440, 2880], P('section', 'expert'), may hold values from -0.15625 to 0.15625
- down: bfloat16 [4, 8, 1440, 1440], P('section', 'expert'), may hold values from -0.15625 to 0.15625
- routes: int32 [4, 6, 192, 4], P('section', None, 'expert'), may hold values from 0 to 7, all different within a row; in each aligned block of 24 rows (0 to 23, 24 to 47, ..., all dimensions but the last counted through in order) at most 18 rows name the same one
- route_weights: int32 [4, 6, 192, 4], P('section', None, 'expert'), may hold values from 1 to 4095
Outputs:
- layer_outputs: bfloat16 [4, 6, 192, 1440], P('section', None, 'expert')
The draws below stay inside these ranges and needn't reach their ends.
Inputs may be any that keep to these rules, and one draw needn't show every extreme that they name: `routes`: each token names 4 different experts; among the 24 tokens of one index of expert in one micro-batch of one layer, no expert is named by more than 18 tokens, a bound that some block reaches.
All inputs are finite; a program needn't handle non-finite values.
Results may differ from the reference program's by a relative error of at most 0.007.
Values may be sent and summed in bfloat16 or wider, within the bound.
A program may use at most 64 MiB of HBM per device.

```python
import math
import jax
import jax.numpy as jnp
import numpy as np
from jax import lax

D = 1440
HID = 1440
TOP = 4
MICRO = 6
TOK_DEV = 24
LAYERS = 4
EXPERTS = 8
TOKENS = 192
CAP = 18
N_EXPERT = 8


def draw_tokens(key, part):
    key_rows, key_cols, key_base = jax.random.split(key, 3)
    low = math.log(0.3)
    high = math.log(3.0)
    row_scale = jnp.exp(jax.random.uniform(key_rows, (MICRO, TOKENS, 1), jnp.float32, low, high))
    col_scale = jnp.exp(jax.random.uniform(key_cols, (1, 1, D), jnp.float32, low, high))
    base = jnp.clip(jax.random.normal(key_base, (MICRO, TOKENS, D), jnp.float32), -4.0, 4.0)
    return (base * row_scale * col_scale).astype(jnp.bfloat16)


def place_ends(entries, rng, smallest, largest):
    longest = entries.shape.index(max(entries.shape))
    spots = []
    for shift in (0, 1):
        where = [jax.random.randint(jax.random.fold_in(rng, axis), (), 0, length) for axis, length in enumerate(entries.shape)]
        where[longest] = (where[longest] + shift) % entries.shape[longest]
        spots.append(tuple(where))
    return entries.at[spots[0]].set(smallest).at[spots[1]].set(largest)


def shard_levels(own_key, dims, shards, smallest, high):
    def one(position, parts):
        draws = jax.random.uniform(jax.random.fold_in(jax.random.fold_in(own_key, 6), position), (parts,), jnp.float32, smallest / len(shards), high / len(shards))
        return jnp.repeat(jnp.exp(draws), dims[position] // parts).reshape((-1,) + (1,) * (len(dims) - position - 1))

    gain = one(*shards[0])
    for cut in shards[1:]:
        gain = gain * one(*cut)
    return gain


def shared_out(stream_key, own, number, rows, number_of, top, reach, lean):
    sequence = jax.random.permutation(stream_key, number_of)
    packed, common = load_shares(number_of, rows * top, reach, lean, True), load_shares(number_of, rows * top, reach, lean, False)
    places = jnp.arange(number_of)

    def named(sizes, offset_by):
        used = int((sizes > 0).sum())
        fixed = max(1, used // 4)
        moved = fixed + (places - fixed + offset_by * (used - fixed)) % max(1, number_of - fixed)
        return jnp.zeros((number_of,), jnp.int32).at[sequence[jnp.where(places < fixed, places, moved)]].set(jnp.asarray(sizes, jnp.int32))

    sizes = jnp.where(number % 4 == 0, named(packed, number // 4), named(common, number - number // 4 - 1))
    mixed = jax.random.permutation(jax.random.fold_in(own, 3), number_of)
    giver, receiver = mixed[0:number_of // 2 * 2:2], mixed[1:number_of // 2 * 2:2]
    margin = jnp.minimum(sizes[giver] - 1, reach - sizes[receiver]) // 2
    margin = jnp.where((giver == sequence[0]) | (receiver == sequence[0]) | (sizes[receiver] == 0), 0, jnp.maximum(margin, 0))
    moved = jax.random.randint(jax.random.fold_in(own, 4), (number_of // 2,), 0, 1 << 20) % (margin + 1)
    sizes = sizes.at[giver].add(-moved).at[receiver].add(moved)
    labels = jnp.searchsorted(jnp.cumsum(sizes), jnp.arange(rows * top), side="right").astype(jnp.int32)
    table = labels.reshape(top, rows).T
    table = table[jax.random.permutation(jax.random.fold_in(own, 1), rows)]
    offset_by = jax.random.randint(jax.random.fold_in(own, 2), (rows, 1), 0, top)
    return jnp.take_along_axis(table, (jnp.arange(top)[None, :] + offset_by) % top, axis=1)


def load_shares(count, total, reach, slope, full):
    loads = [(1 << 20) // math.isqrt(rank ** slope) + 1 for rank in range(1, count + 1)]
    largest = reach if full else min(reach, max(-(-total // count), total * loads[0] // sum(loads)))
    least = 1 if total - largest >= count - 1 else 0
    holding, rest = [largest] + [least] * (count - 1), total - largest - least * (count - 1)
    while rest > 0:
        free = [i for i in range(1, count) if holding[i] < largest] or [i for i in range(1, count) if holding[i] < reach]
        pool, budget = sum([loads[i] for i in free]), rest
        for i in free:
            addition = min(reach - holding[i], max(1, budget * loads[i] // pool), rest)
            holding[i] = holding[i] + addition
            rest = rest - addition
    return np.array(holding)


def bell_draw(own_key, dims, spread, limit, cuts=(), kind=jnp.bfloat16):
    drawn = spread * jax.random.normal(own_key, dims, jnp.float32)
    if cuts:
        drawn = drawn * shard_levels(own_key, dims, cuts, -0.22, 0.18)
    return jnp.clip(drawn, -limit, limit).astype(kind)


def setup_inputs(seed: int = 0) -> dict:
    keys = jax.random.split(jax.random.key(seed), 7)
    tokens = draw_tokens(jax.random.fold_in(keys[6], 71), 0)
    norm_gain = jnp.clip(1.0 + 0.1 * jax.random.normal(keys[1], (LAYERS, D), jnp.float32), 0.5, 1.5)
    gate_up = bell_draw(keys[2], (LAYERS, EXPERTS, D, 2 * HID), D ** -0.5, 0.15625, ((0, 4), (1, 8)))
    down = bell_draw(keys[3], (LAYERS, EXPERTS, HID, D), HID ** -0.5, 0.15625, ((0, 4), (1, 8)))
    routes_keys = jax.random.split(jax.random.fold_in(keys[4], 1), LAYERS * MICRO * TOKENS // TOK_DEV)
    routes_turns = jax.random.permutation(jax.random.fold_in(keys[4], 3), LAYERS * MICRO * TOKENS // TOK_DEV)
    routes = jax.vmap(lambda own, number: shared_out(jax.random.fold_in(keys[4], 2), own, number, TOK_DEV, EXPERTS, TOP, CAP, 2))(routes_keys, routes_turns).reshape((LAYERS, MICRO, TOKENS, TOP))
    route_weights = place_ends(jax.random.randint(keys[5], (LAYERS, MICRO, TOKENS, TOP), 1, 4096), jax.random.fold_in(keys[5], 1), 1, 4095).astype(jnp.int32)
    return dict(tokens=tokens, norm_gain=norm_gain, gate_up=gate_up, down=down, routes=routes, route_weights=route_weights)


def expert_rows(normed_rows, flat_routes, gate_up_layer, down_layer):
    row_count = normed_rows.shape[0]
    bound = N_EXPERT * CAP

    def one_expert(outcome, which):
        positions = jnp.nonzero(flat_routes == which, size=bound, fill_value=row_count)[0].astype(jnp.int32)
        picked = jnp.take(normed_rows, jnp.minimum(positions, row_count - 1), axis=0)
        projected = jnp.dot(picked, gate_up_layer[which], preferred_element_type=jnp.float32)
        gate_part = projected[:, :HID]
        up_part = projected[:, HID:]
        activated = (gate_part * jax.nn.sigmoid(1.702 * gate_part) * (up_part + 1.0)).astype(jnp.bfloat16)
        result_rows = jnp.dot(activated, down_layer[which], preferred_element_type=jnp.float32).astype(jnp.bfloat16)
        outcome = outcome.at[positions].set(result_rows.astype(outcome.dtype), mode='drop')
        return (outcome, None)
    start = jnp.zeros((row_count, D), normed_rows.dtype)
    outcome, unused = lax.scan(one_expert, start, jnp.arange(EXPERTS, dtype=jnp.int32))
    return outcome

def reference(tokens, norm_gain, gate_up, down, routes, route_weights):
    current = [tokens[micro_index] for micro_index in range(MICRO)]
    layers_out = []
    for layer in range(LAYERS):
        results = []
        for micro_index in range(MICRO):
            stream = current[micro_index].astype(jnp.float32)
            scale = lax.rsqrt(lax.optimization_barrier(jnp.mean(stream * stream, axis=-1, keepdims=True)) + 1e-05)
            normed = (stream * scale * norm_gain[layer][None, :].astype(jnp.float32)).astype(jnp.bfloat16)
            repeated = jnp.repeat(normed, TOP, axis=0)
            flat_routes = routes[layer, micro_index].reshape(-1)
            expert_out = expert_rows(repeated, flat_routes, gate_up[layer], down[layer]).reshape(TOKENS, TOP, D)
            fixed_point = route_weights[layer, micro_index].astype(jnp.float32)
            shares = fixed_point / lax.optimization_barrier(jnp.sum(fixed_point, axis=-1, keepdims=True))
            mixed = stream + lax.optimization_barrier(jnp.sum(shares[:, :, None] * expert_out.astype(jnp.float32), axis=1))
            results.append(mixed.astype(jnp.bfloat16))
        current = results
        layers_out.append(jnp.stack(results))
    return jnp.stack(layers_out)
```

```python
import functools

import jax
import jax.numpy as jnp
from jax import lax
from jax.experimental import pallas as pl
from jax.experimental.pallas import tpu as pltpu
from jax.sharding import PartitionSpec as P

F32 = jnp.float32
BF16 = jnp.bfloat16
LANES = 128
CORES = 2
CHUNK = 256
VMEM_BYTES = 56 * 2**20


def passed_along(value, axis, steps):
    count = lax.axis_size(axis)
    leading, last = (max(0, -steps), min(count, count - steps))
    return lax.ppermute(value, axis, [(source, source + steps) for source in range(leading, last)])


def expert_ffn(arrived, gate_up_w, down_w):
    senders, slot_count, width = arrived.shape
    hidden_units = down_w.shape[0]
    flat_rows = arrived.reshape(senders * slot_count, width)
    projected = jnp.dot(flat_rows, gate_up_w, preferred_element_type=jnp.float32)
    gate_part = projected[:, :hidden_units]
    up_part = projected[:, hidden_units:]
    activated = (gate_part * jax.nn.sigmoid(1.702 * gate_part) * (up_part + 1.0)).astype(
        jnp.bfloat16
    )
    result_rows = jnp.dot(activated, down_w, preferred_element_type=jnp.float32).astype(
        jnp.bfloat16
    )
    return result_rows.reshape(senders, slot_count, width)


def layer_step(stream, gain_row, gate_up_w, down_w, route_rows, weight_rows):
    token_count, chosen = route_rows.shape
    width = stream.shape[1]
    experts_n = lax.axis_size("expert")
    capacity = max(2, token_count * chosen * 3 // (2 * experts_n))
    widened = stream.astype(jnp.float32)
    scale = lax.rsqrt(jnp.mean(widened * widened, axis=-1, keepdims=True) + 1e-05)
    normed = (widened * scale * gain_row[None, :]).astype(jnp.bfloat16)
    flat_routes = route_rows.reshape(-1)
    matches = (flat_routes[:, None] == jnp.arange(experts_n, dtype=jnp.int32)[None, :]).astype(
        jnp.int32
    )
    slot_index = jnp.sum((jnp.cumsum(matches, axis=0) - 1) * matches, axis=1)
    target = flat_routes * capacity + slot_index
    placing = (
        jnp.arange(experts_n * capacity, dtype=jnp.int32)[:, None] == target[None, :]
    ).astype(jnp.bfloat16)
    repeated = jnp.repeat(normed, chosen, axis=0)
    outgoing = jnp.dot(placing, repeated, preferred_element_type=jnp.float32).astype(jnp.bfloat16)
    outgoing = outgoing.reshape(experts_n, capacity, width)
    arrived = lax.all_to_all(outgoing, "expert", split_axis=0, concat_axis=0, tiled=True)
    computed = expert_ffn(arrived, gate_up_w, down_w)
    returned = lax.all_to_all(computed, "expert", split_axis=0, concat_axis=0, tiled=True)
    returned_rows = returned.reshape(experts_n * capacity, width)
    gathered = jnp.take(returned_rows, target, axis=0).reshape(token_count, chosen, width)
    fixed_point = weight_rows.astype(jnp.float32)
    shares = fixed_point / jnp.sum(fixed_point, axis=-1, keepdims=True)
    accumulated = widened
    for branch in range(chosen):
        accumulated = accumulated + shares[:, branch : branch + 1] * gathered[:, branch].astype(
            jnp.float32
        )
    return accumulated.astype(jnp.bfloat16)


def ticked_shards(tokens, norm_gain, gate_up, down, routes, route_weights):
    micro_count, token_count, width = tokens.shape
    sections = lax.axis_size("section")
    section_index = lax.axis_index("section")
    gain_row = norm_gain[0]
    gate_up_w = gate_up[0, 0]
    down_w = down[0, 0]
    incoming = jnp.zeros((token_count, width), jnp.bfloat16)
    results = jnp.zeros((micro_count, token_count, width), jnp.bfloat16)
    tick_total = micro_count + sections - 1
    for tick_number in range(tick_total):
        fresh_input = tokens[min(tick_number, micro_count - 1)]
        stream = jnp.where(section_index == 0, fresh_input, incoming)
        micro_here = tick_number - section_index
        clamped = jnp.clip(micro_here, 0, micro_count - 1)
        route_rows = lax.dynamic_index_in_dim(routes[0], clamped, 0, keepdims=False)
        weight_rows = lax.dynamic_index_in_dim(route_weights[0], clamped, 0, keepdims=False)
        output_rows = layer_step(stream, gain_row, gate_up_w, down_w, route_rows, weight_rows)
        active = jnp.logical_and(micro_here >= 0, micro_here < micro_count)
        updated = lax.dynamic_update_index_in_dim(results, output_rows, clamped, 0)
        results = jnp.where(active, updated, results)
        if tick_number + 1 < tick_total:
            incoming = passed_along(output_rows, "section", 1)
    return results[None]


def folded(rows, half):
    token_count, width = rows.shape
    rest = jnp.concatenate(
        [rows[:, half:], jnp.zeros((token_count, 2 * half - width), rows.dtype)], axis=1
    )
    return jnp.concatenate([rows[:, :half], rest], axis=0)


def kernel(
    dims,
    tokens_ref, gain_ref, gate_up_hbm, down_hbm, routes_ref, weights_ref,
    out_ref,
    gate_up_w, up_w, down_w, stream, blocks, rows_x, rows_act, partial, sib_out, sib_in,
    sum_out, sum_in, passed,
    weight_sem, lane_send, lane_recv, fwd_send, sib_send, sib_recv, sum_send, sum_recv,
    pass_send, pass_recv,
):
    sections, experts, micros, token_count, width, hidden, half = dims
    chips = experts // CORES
    second = width - half
    tile = second // LANES * LANES
    spot = second - tile
    section, me = lax.axis_index("section"), lax.axis_index("expert")
    chip, core = me // CORES, me % CORES
    sibling = chip * CORES + 1 - core

    loads = [
        pltpu.make_async_copy(gate_up_hbm.at[0, 0], gate_up_w, weight_sem.at[0]),
        pltpu.make_async_copy(down_hbm.at[0, 0], down_w, weight_sem.at[1]),
    ]
    for load in loads:
        load.start()

    def other(step):
        return lax.rem(chip + step, chips)

    def to(src, dst, send, recv, expert, sec=section):
        return pltpu.make_async_remote_copy(
            src_ref=src, dst_ref=dst, send_sem=send, recv_sem=recv,
            device_id=(sec, expert), device_id_type=pl.DeviceIdType.MESH,
        )

    barrier = pltpu.get_barrier_semaphore()
    for step in range(1, chips):
        pl.semaphore_signal(
            barrier, inc=1, device_id=(section, other(step) * CORES + core),
            device_id_type=pl.DeviceIdType.MESH,
        )
    pl.semaphore_signal(
        barrier, inc=1, device_id=(section, sibling), device_id_type=pl.DeviceIdType.MESH
    )

    @pl.when(section > 0)
    def _():
        pl.semaphore_signal(
            barrier, inc=1, device_id=(section - 1, me), device_id_type=pl.DeviceIdType.MESH
        )

    pl.semaphore_wait(barrier, chips + jnp.where(section + 1 < sections, 1, 0))

    @pl.when(section == 0)
    def _():
        for m in range(micros):
            stream[m] = folded(tokens_ref[m].astype(F32), half).astype(BF16)

    gain = folded(gain_ref[...], half)

    def lane_copy(m, step):
        return to(
            blocks.at[m, me], blocks.at[m, me], lane_send.at[m, step], lane_recv.at[m, me],
            other(step) * CORES + core,
        )

    def sibling_copy(m, owner, step):
        return to(
            blocks.at[m, owner], blocks.at[m, owner], fwd_send.at[m, step],
            lane_recv.at[m, owner], sibling,
        )

    def partial_copy(m):
        return to(sib_out.at[m], sib_in.at[m], sib_send.at[m], sib_recv.at[m], sibling)

    def sum_copy(m, step):
        there = other(step)
        return to(
            sum_out.at[m, there], sum_in.at[m, chip], sum_send.at[m, step],
            sum_recv.at[m, chip], there * CORES + core,
        )

    def pass_copy(m):
        return to(
            passed.at[m], stream.at[m], pass_send.at[m], pass_recv.at[m], me,
            lax.rem(section + 1, sections),
        )

    def got_block(m, owner):
        to(
            blocks.at[m, owner], blocks.at[m, owner], fwd_send.at[m, 0],
            lane_recv.at[m, owner], sibling,
        ).wait_recv()

    def send_rows(m):
        @pl.when(section > 0)
        def _():
            pass_copy(m).wait_recv()

        both = stream[m].astype(F32)
        low, high = both[:token_count], both[token_count:]
        squares = jnp.sum(low * low, axis=-1, keepdims=True) + jnp.sum(
            high * high, axis=-1, keepdims=True
        )
        scale = lax.rsqrt(squares / width + 1e-05)
        low = low * scale * gain[:1]
        high = high * scale * gain[1:]
        route_rows = routes_ref[0, m]
        fixed_point = weights_ref[0, m].astype(F32)
        shares = fixed_point / jnp.sum(fixed_point, axis=-1, keepdims=True)
        lane = lax.broadcasted_iota(jnp.int32, (token_count, LANES), 1) - spot
        first = jnp.zeros((token_count, LANES), F32)
        again = jnp.zeros((token_count, LANES), F32)
        for k in range(route_rows.shape[1]):
            named, share = route_rows[:, k : k + 1], shares[:, k : k + 1]
            first = first + jnp.where(named == lane, share, 0.0)
            again = again + jnp.where(named == lane - experts, share, 0.0)
        rest = again - again.astype(BF16).astype(F32)
        last = high[:, tile:] + first + rest
        high = last if tile == 0 else jnp.concatenate([high[:, :tile], last], axis=1)
        blocks[m, me] = jnp.concatenate([low, high], axis=0).astype(BF16)
        for step in range(1, chips):
            lane_copy(m, step).start()
        sibling_copy(m, me, 0).start()

    def forward_rows(m):
        for step in range(1, chips):
            owner = other(step) * CORES + core
            got_block(m, owner)
            sibling_copy(m, owner, step).start()

    def compute(m):
        for step in range(chips):
            got_block(m, other(step) * CORES + 1 - core)
        rows = experts * token_count
        arrived = blocks[m].astype(F32)
        low = arrived[:, :token_count].reshape(rows, half)
        high = arrived[:, token_count:].reshape(rows, half)
        lane = lax.broadcasted_iota(jnp.int32, (rows, LANES), 1) - spot
        mine = jnp.logical_or(lane == me, lane == me + experts)
        share = jnp.sum(jnp.where(mine, high[:, tile:], 0.0), axis=-1, keepdims=True)
        rows_x[:, :half] = low.astype(BF16)
        rows_x[:, half:] = high.astype(BF16)
        x = rows_x[:, :width]
        for at in range(0, hidden, CHUNK):
            upto = min(at + CHUNK, hidden)
            gate = jnp.dot(x, gate_up_w[:, at:upto], preferred_element_type=F32)
            up = jnp.dot(x, up_w[:, at:upto], preferred_element_type=F32)
            rows_act[:, at:upto] = (gate * jax.nn.sigmoid(1.702 * gate) * (up + 1.0)).astype(BF16)
        act = rows_act[:, :hidden]
        for at in [*range(0, half, CHUNK), *range(half, width, CHUNK)]:
            end = half if at < half else 2 * half
            room = min(CHUNK, end - at)
            upto = min(at + room, width)
            value = jnp.dot(act, down_w[:, at:upto], preferred_element_type=F32) * share
            if upto - at < room:
                value = jnp.concatenate(
                    [value, jnp.zeros((rows, room - (upto - at)), F32)], axis=1
                )
            value = value.reshape(chips, CORES, token_count, room)
            top = 0 if at < half else token_count
            left = at if at < half else at - half
            for c in range(CORES):
                partial[c, :, top : top + token_count, left : left + room] = value[:, c]

    def add_siblings(m):
        sib_out[m] = partial[1 - core].astype(BF16)
        partial_copy(m).start()

    def send_sums(m):
        partial_copy(m).wait_recv()
        for step in range(chips - 1, 0, -1):
            there = other(step)
            total = partial[core, there] + sib_in[m, there].astype(F32)
            sum_out[m, there] = total.astype(BF16)
            sum_copy(m, step).start()

    def finish(m):
        total = stream[m].astype(F32) + partial[core, chip] + sib_in[m, chip].astype(F32)
        for step in range(1, chips):
            there = other(step)
            to(
                sum_out.at[m, there], sum_in.at[m, there], sum_send.at[m, step],
                sum_recv.at[m, there], there * CORES + core,
            ).wait_recv()
            total = total + sum_in[m, there].astype(F32)
        passed[m] = total.astype(BF16)

        @pl.when(section + 1 < sections)
        def _():
            pass_copy(m).start()

        out_ref[0, m] = jnp.concatenate(
            [total[:token_count], total[token_count:, :second]], axis=1
        ).astype(BF16)

    send_rows(0)
    loads[0].wait()

    def realign(i, carry):
        at = pl.ds(pl.multiple_of(i * 32, 32), 32)
        up_w[at, :] = gate_up_w[at, hidden:]
        return carry

    lax.fori_loop(0, width // 32, realign, 0)
    loads[1].wait()
    forward_rows(0)

    def step_over(m, carry):
        compute(m)
        add_siblings(m)
        send_sums(m)

        @pl.when(m + 1 < micros)
        def _():
            send_rows(m + 1)

        finish(m)

        @pl.when(m + 1 < micros)
        def _():
            forward_rows(m + 1)

        return carry

    lax.fori_loop(0, micros, step_over, 0)

    def drain(m, carry):
        for step in range(1, chips):
            lane_copy(m, step).wait_send()
            sum_copy(m, step).wait_send()
        for step in range(chips):
            sibling_copy(m, me, step).wait_send()
        partial_copy(m).wait_send()

        @pl.when(section + 1 < sections)
        def _():
            pass_copy(m).wait_send()

        return carry

    lax.fori_loop(0, micros, drain, 0)


def half_width(width):
    tiles = -(-width // LANES)
    return -(-tiles // 2) * LANES


def fits_vmem(sections, experts, micros, token_count, width, hidden):
    half = half_width(width)
    chips = experts // CORES
    block = 2 * token_count * half * 2
    held = micros * block * (experts + 3 * chips + 3) + 2 * experts * block
    held += (2 * hidden + 4 * LANES) * width * 4
    room = (width - half) % LANES + 2 * experts <= LANES and width < 2 * half
    rows_ok = token_count % 8 == 0 and width % 32 == 0 and hidden % 32 == 0
    return experts % CORES == 0 and experts > CORES and room and rows_ok and held < 32 * 2**20


def whole_kernel(tokens, norm_gain, gate_up, down, routes, route_weights):
    micros, token_count, width = tokens.shape
    hidden = down.shape[2]
    sections, experts = lax.axis_size("section"), lax.axis_size("expert")
    half = half_width(width)
    chips = experts // CORES
    dims = (sections, experts, micros, token_count, width, hidden, half)
    folded_rows = 2 * token_count
    rows = experts * token_count
    dma = pltpu.SemaphoreType.DMA
    vmem = pl.BlockSpec(memory_space=pltpu.VMEM)
    hbm = pl.BlockSpec(memory_space=pl.ANY)
    work = 6 * micros * rows * width * hidden
    return pl.pallas_call(
        functools.partial(kernel, dims),
        out_shape=jax.ShapeDtypeStruct((1, micros, token_count, width), BF16),
        in_specs=[vmem, vmem, hbm, hbm, vmem, vmem],
        out_specs=vmem,
        scratch_shapes=[
            pltpu.VMEM((width, 2 * hidden), BF16),
            pltpu.VMEM((width, hidden), BF16),
            pltpu.VMEM((hidden, width), BF16),
            pltpu.VMEM((micros, folded_rows, half), BF16),
            pltpu.VMEM((micros, experts, folded_rows, half), BF16),
            pltpu.VMEM((rows, 2 * half), BF16),
            pltpu.VMEM((rows, hidden), BF16),
            pltpu.VMEM((CORES, chips, folded_rows, half), F32),
            pltpu.VMEM((micros, chips, folded_rows, half), BF16),
            pltpu.VMEM((micros, chips, folded_rows, half), BF16),
            pltpu.VMEM((micros, chips, folded_rows, half), BF16),
            pltpu.VMEM((micros, chips, folded_rows, half), BF16),
            pltpu.VMEM((micros, folded_rows, half), BF16),
            dma((2,)),
            dma((micros, chips)),
            dma((micros, experts)),
            dma((micros, chips)),
            dma((micros,)),
            dma((micros,)),
            dma((micros, chips)),
            dma((micros, chips)),
            dma((micros,)),
            dma((micros,)),
        ],
        compiler_params=pltpu.CompilerParams(
            collective_id=0, has_side_effects=True, vmem_limit_bytes=VMEM_BYTES
        ),
        cost_estimate=pl.CostEstimate(
            flops=work, bytes_accessed=6 * width * hidden, transcendentals=micros * rows * hidden
        ),
    )(tokens, norm_gain, gate_up, down, routes, route_weights)


def solution(mesh):
    sections, experts = mesh.shape["section"], mesh.shape["expert"]

    def shards(tokens, norm_gain, gate_up, down, routes, route_weights):
        micros, token_count, width = tokens.shape
        hidden = down.shape[2]
        if fits_vmem(sections, experts, micros, token_count, width, hidden):
            return whole_kernel(tokens, norm_gain, gate_up, down, routes, route_weights)
        return ticked_shards(tokens, norm_gain, gate_up, down, routes, route_weights)

    return jax.shard_map(
        shards,
        mesh=mesh,
        in_specs=(
            P(None, "expert", None),
            P("section", None),
            P("section", "expert", None, None),
            P("section", "expert", None, None),
            P("section", None, "expert", None),
            P("section", None, "expert", None),
        ),
        out_specs=P("section", None, "expert", None),
        check_vma=False,
    )
```

```python
import functools

import jax
import jax.numpy as jnp
from jax import lax
from jax.experimental import pallas as pl
from jax.experimental.pallas import tpu as pltpu
from jax.sharding import PartitionSpec as P

F32 = jnp.float32
BF16 = jnp.bfloat16
LANES = 128
CORES = 2
CHUNK = 256
VMEM_BYTES = 56 * 2**20


def passed_along(value, axis, steps):
    count = lax.axis_size(axis)
    leading, last = (max(0, -steps), min(count, count - steps))
    return lax.ppermute(value, axis, [(source, source + steps) for source in range(leading, last)])


def expert_ffn(arrived, gate_up_w, down_w):
    senders, slot_count, width = arrived.shape
    hidden_units = down_w.shape[0]
    flat_rows = arrived.reshape(senders * slot_count, width)
    projected = jnp.dot(flat_rows, gate_up_w, preferred_element_type=jnp.float32)
    gate_part = projected[:, :hidden_units]
    up_part = projected[:, hidden_units:]
    activated = (gate_part * jax.nn.sigmoid(1.702 * gate_part) * (up_part + 1.0)).astype(
        jnp.bfloat16
    )
    result_rows = jnp.dot(activated, down_w, preferred_element_type=jnp.float32).astype(
        jnp.bfloat16
    )
    return result_rows.reshape(senders, slot_count, width)


def layer_step(stream, gain_row, gate_up_w, down_w, route_rows, weight_rows):
    token_count, chosen = route_rows.shape
    width = stream.shape[1]
    experts_n = lax.axis_size("expert")
    capacity = max(2, token_count * chosen * 3 // (2 * experts_n))
    widened = stream.astype(jnp.float32)
    scale = lax.rsqrt(jnp.mean(widened * widened, axis=-1, keepdims=True) + 1e-05)
    normed = (widened * scale * gain_row[None, :]).astype(jnp.bfloat16)
    flat_routes = route_rows.reshape(-1)
    matches = (flat_routes[:, None] == jnp.arange(experts_n, dtype=jnp.int32)[None, :]).astype(
        jnp.int32
    )
    slot_index = jnp.sum((jnp.cumsum(matches, axis=0) - 1) * matches, axis=1)
    target = flat_routes * capacity + slot_index
    placing = (
        jnp.arange(experts_n * capacity, dtype=jnp.int32)[:, None] == target[None, :]
    ).astype(jnp.bfloat16)
    repeated = jnp.repeat(normed, chosen, axis=0)
    outgoing = jnp.dot(placing, repeated, preferred_element_type=jnp.float32).astype(jnp.bfloat16)
    outgoing = outgoing.reshape(experts_n, capacity, width)
    arrived = lax.all_to_all(outgoing, "expert", split_axis=0, concat_axis=0, tiled=True)
    computed = expert_ffn(arrived, gate_up_w, down_w)
    returned = lax.all_to_all(computed, "expert", split_axis=0, concat_axis=0, tiled=True)
    returned_rows = returned.reshape(experts_n * capacity, width)
    gathered = jnp.take(returned_rows, target, axis=0).reshape(token_count, chosen, width)
    fixed_point = weight_rows.astype(jnp.float32)
    shares = fixed_point / jnp.sum(fixed_point, axis=-1, keepdims=True)
    accumulated = widened
    for branch in range(chosen):
        accumulated = accumulated + shares[:, branch : branch + 1] * gathered[:, branch].astype(
            jnp.float32
        )
    return accumulated.astype(jnp.bfloat16)


def ticked_shards(tokens, norm_gain, gate_up, down, routes, route_weights):
    micro_count, token_count, width = tokens.shape
    sections = lax.axis_size("section")
    section_index = lax.axis_index("section")
    gain_row = norm_gain[0]
    gate_up_w = gate_up[0, 0]
    down_w = down[0, 0]
    incoming = jnp.zeros((token_count, width), jnp.bfloat16)
    results = jnp.zeros((micro_count, token_count, width), jnp.bfloat16)
    tick_total = micro_count + sections - 1
    for tick_number in range(tick_total):
        fresh_input = tokens[min(tick_number, micro_count - 1)]
        stream = jnp.where(section_index == 0, fresh_input, incoming)
        micro_here = tick_number - section_index
        clamped = jnp.clip(micro_here, 0, micro_count - 1)
        route_rows = lax.dynamic_index_in_dim(routes[0], clamped, 0, keepdims=False)
        weight_rows = lax.dynamic_index_in_dim(route_weights[0], clamped, 0, keepdims=False)
        output_rows = layer_step(stream, gain_row, gate_up_w, down_w, route_rows, weight_rows)
        active = jnp.logical_and(micro_here >= 0, micro_here < micro_count)
        updated = lax.dynamic_update_index_in_dim(results, output_rows, clamped, 0)
        results = jnp.where(active, updated, results)
        if tick_number + 1 < tick_total:
            incoming = passed_along(output_rows, "section", 1)
    return results[None]


def folded(rows, half):
    token_count, width = rows.shape
    rest = jnp.concatenate(
        [rows[:, half:], jnp.zeros((token_count, 2 * half - width), rows.dtype)], axis=1
    )
    return jnp.concatenate([rows[:, :half], rest], axis=0)


def kernel(
    dims,
    tokens_ref, gain_ref, gate_up_hbm, down_hbm, routes_ref, weights_ref,
    out_ref,
    gate_up_w, up_w, down_w, stream, blocks, rows_x, rows_act, partial, sib_out, sib_in,
    sum_out, sum_in, passed, share_lanes,
    weight_sem, up_send, low_send, lane_recv, fwd_send, sib_send, sib_recv, sum_send, sum_recv,
    pass_send, pass_recv,
):
    sections, experts, micros, token_count, width, hidden, half = dims
    chips = experts // CORES
    second = width - half
    tile = second // LANES * LANES
    spot = second - tile
    section, me = lax.axis_index("section"), lax.axis_index("expert")
    chip, core = me // CORES, me % CORES
    sibling = chip * CORES + 1 - core

    loads = [
        pltpu.make_async_copy(gate_up_hbm.at[0, 0], gate_up_w, weight_sem.at[0]),
        pltpu.make_async_copy(down_hbm.at[0, 0], down_w, weight_sem.at[1]),
    ]
    for load in loads:
        load.start()

    def other(step):
        return lax.rem(chip + step, chips)

    def to(src, dst, send, recv, expert, sec=section):
        return pltpu.make_async_remote_copy(
            src_ref=src, dst_ref=dst, send_sem=send, recv_sem=recv,
            device_id=(sec, expert), device_id_type=pl.DeviceIdType.MESH,
        )

    barrier = pltpu.get_barrier_semaphore()
    for step in range(1, chips):
        pl.semaphore_signal(
            barrier, inc=1, device_id=(section, other(step) * CORES + core),
            device_id_type=pl.DeviceIdType.MESH,
        )
    pl.semaphore_signal(
        barrier, inc=1, device_id=(section, sibling), device_id_type=pl.DeviceIdType.MESH
    )

    @pl.when(section > 0)
    def _():
        pl.semaphore_signal(
            barrier, inc=1, device_id=(section - 1, me), device_id_type=pl.DeviceIdType.MESH
        )

    pl.semaphore_wait(barrier, chips + jnp.where(section + 1 < sections, 1, 0))

    @pl.when(section == 0)
    def _():
        for m in range(micros):
            stream[m] = folded(tokens_ref[m].astype(F32), half).astype(BF16)

    gain = folded(gain_ref[...], half)

    def up_copy(m, hop):
        owner = (chip - hop) * CORES + core
        return to(
            blocks.at[m, owner], blocks.at[m, owner], up_send.at[m, hop],
            lane_recv.at[m, owner], me + CORES,
        )

    def low_copy(m, hop):
        owner = (chip + hop) * CORES + core
        return to(
            blocks.at[m, owner], blocks.at[m, owner], low_send.at[m, hop],
            lane_recv.at[m, owner], me - CORES,
        )

    def sibling_copy(m, owner):
        return to(
            blocks.at[m, owner], blocks.at[m, owner], fwd_send.at[m, owner // CORES],
            lane_recv.at[m, owner], sibling,
        )

    def partial_copy(m, part):
        return to(
            sib_out.at[m, part], sib_in.at[m, part], sib_send.at[m, part],
            sib_recv.at[m, part], sibling,
        )

    def sum_copy(m, step):
        there = other(step)
        return to(
            sum_out.at[m, there], sum_in.at[m, chip], sum_send.at[m, step],
            sum_recv.at[m, chip], there * CORES + core,
        )

    def pass_copy(m):
        return to(
            passed.at[m], stream.at[m], pass_send.at[m], pass_recv.at[m], me,
            lax.rem(section + 1, sections),
        )

    def got_block(m, owner):
        sibling_copy(m, owner).wait_recv()

    def prepare_shares(m):
        route_rows = routes_ref[0, m]
        fixed_point = weights_ref[0, m].astype(F32)
        shares = fixed_point / jnp.sum(fixed_point, axis=0, keepdims=True)
        lane = lax.broadcasted_iota(jnp.int32, (token_count, LANES), 1) - spot
        square = (token_count, token_count)
        same = lax.broadcasted_iota(jnp.int32, square, 0) == lax.broadcasted_iota(
            jnp.int32, square, 1
        )
        first = jnp.zeros((token_count, LANES), F32)
        again = jnp.zeros((token_count, LANES), F32)
        for k in range(route_rows.shape[0]):
            named = jnp.sum(
                jnp.where(same, route_rows[k : k + 1].astype(F32), 0.0), axis=1, keepdims=True
            ).astype(jnp.int32)
            share = jnp.sum(jnp.where(same, shares[k : k + 1], 0.0), axis=1, keepdims=True)
            first = first + jnp.where(named == lane, share, 0.0)
            again = again + jnp.where(named == lane - experts, share, 0.0)
        rest = again - again.astype(BF16).astype(F32)
        share_lanes[m] = first + rest

    def send_rows(m):
        @pl.when(section > 0)
        def _():
            pass_copy(m).wait_recv()

        both = stream[m].astype(F32)
        low, high = both[:token_count], both[token_count:]
        squares = jnp.sum(low * low, axis=-1, keepdims=True) + jnp.sum(
            high * high, axis=-1, keepdims=True
        )
        scale = lax.rsqrt(squares / width + 1e-05)
        low = low * scale * gain[:1]
        high = high * scale * gain[1:]
        last = high[:, tile:] + share_lanes[m]
        high = last if tile == 0 else jnp.concatenate([high[:, :tile], last], axis=1)
        blocks[m, me] = jnp.concatenate([low, high], axis=0).astype(BF16)
        pass_block(m, 0)

    def pass_block(m, hop):
        @pl.when(jnp.logical_and(chip >= hop, chip + 1 < chips))
        def _():
            up_copy(m, hop).start()

        @pl.when(jnp.logical_and(chip + hop < chips, chip > 0))
        def _():
            low_copy(m, hop).start()

        if hop == 0:
            sibling_copy(m, me).start()

    def relay(m, hop):
        @pl.when(chip >= hop)
        def _():
            owner = (chip - hop) * CORES + core
            got_block(m, owner)

            @pl.when(chip + 1 < chips)
            def _():
                up_copy(m, hop).start()

            sibling_copy(m, owner).start()

        @pl.when(chip + hop < chips)
        def _():
            owner = (chip + hop) * CORES + core
            got_block(m, owner)

            @pl.when(chip > 0)
            def _():
                low_copy(m, hop).start()

            sibling_copy(m, owner).start()

    def project(m, between):
        for step in range(chips):
            got_block(m, other(step) * CORES + 1 - core)
        rows = experts * token_count
        arrived = blocks[m].astype(F32)
        low = arrived[:, :token_count].reshape(rows, half)
        high = arrived[:, token_count:].reshape(rows, half)
        lane = lax.broadcasted_iota(jnp.int32, (rows, LANES), 1) - spot
        mine = jnp.logical_or(lane == me, lane == me + experts)
        share = jnp.sum(jnp.where(mine, high[:, tile:], 0.0), axis=-1, keepdims=True)
        rows_x[:, :half] = low.astype(BF16)
        rows_x[:, half:] = high.astype(BF16)
        x = rows_x[:, :width]
        for at in range(0, hidden, CHUNK):
            upto = min(at + CHUNK, hidden)
            gate = jnp.dot(x, gate_up_w[:, at:upto], preferred_element_type=F32)
            up = jnp.dot(x, up_w[:, at:upto], preferred_element_type=F32)
            rows_act[:, at:upto] = (gate * jax.nn.sigmoid(1.702 * gate) * (up + 1.0)).astype(BF16)
            if at <= hidden // 3 < upto:
                between()
        return share

    def bring_down(m, part, share):
        act = rows_act[:, :hidden]
        rows = experts * token_count
        for left in range(0, half, CHUNK):
            at = part * half + left
            room = min(CHUNK, half - left)
            upto = min(at + room, width)
            value = jnp.dot(act, down_w[:, at:upto], preferred_element_type=F32) * share
            if upto - at < room:
                value = jnp.concatenate(
                    [value, jnp.zeros((rows, room - (upto - at)), F32)], axis=1
                )
            value = value.reshape(chips, CORES, token_count, room)
            for c in range(CORES):
                partial[c, part, :, left : left + room] = value[:, c].reshape(-1, room)
        sib_out[m, part] = partial[1 - core, part].astype(BF16)
        partial_copy(m, part).start()

    def own_sum(there):
        at = pl.ds(pl.multiple_of(there * token_count, 8), token_count)
        return jnp.concatenate([partial[core, 0, at, :], partial[core, 1, at, :]], axis=0)

    def send_sums(m):
        for part in range(2):
            partial_copy(m, part).wait_recv()
            partial[core, part] = partial[core, part] + sib_in[m, part].astype(F32)
        for step in range(chips - 1, 0, -1):
            there = other(step)
            sum_out[m, there] = own_sum(there).astype(BF16)
            sum_copy(m, step).start()

    def finish(m):
        total = stream[m].astype(F32) + own_sum(chip)
        for step in range(1, chips):
            there = other(step)
            to(
                sum_out.at[m, there], sum_in.at[m, there], sum_send.at[m, step],
                sum_recv.at[m, there], there * CORES + core,
            ).wait_recv()
            total = total + sum_in[m, there].astype(F32)
        passed[m] = total.astype(BF16)

        @pl.when(section + 1 < sections)
        def _():
            pass_copy(m).start()

        out_ref[0, m] = jnp.concatenate(
            [total[:token_count], total[token_count:, :second]], axis=1
        ).astype(BF16)

    def prepare(m, carry):
        prepare_shares(m)
        return carry

    prepare_shares(0)
    send_rows(0)
    lax.fori_loop(1, micros, prepare, 0)
    loads[0].wait()

    def realign(i, carry):
        at = pl.ds(pl.multiple_of(i * 32, 32), 32)
        up_w[at, :] = gate_up_w[at, hidden:]
        return carry

    lax.fori_loop(0, width // 32, realign, 0)
    loads[1].wait()
    for hop in range(1, chips):
        relay(0, hop)

    def step_over(m, carry):
        def ahead(work):
            pl.when(m + 1 < micros)(work)

        share = project(m, lambda: ahead(lambda: send_rows(m + 1)))

        @pl.when(m > 0)
        def _():
            finish(m - 1)

        bring_down(m, 0, share)
        ahead(lambda: relay(m + 1, 1))
        bring_down(m, 1, share)
        if chips > 2:
            ahead(lambda: relay(m + 1, 2))
        send_sums(m)
        for hop in range(3, chips):
            ahead(functools.partial(relay, m + 1, hop))
        return carry

    lax.fori_loop(0, micros, step_over, 0)
    finish(micros - 1)

    def drain(m, carry):
        for hop in range(chips):
            @pl.when(jnp.logical_and(chip >= hop, chip + 1 < chips))
            def _():
                up_copy(m, hop).wait_send()

            @pl.when(jnp.logical_and(chip + hop < chips, chip > 0))
            def _():
                low_copy(m, hop).wait_send()

            sibling_copy(m, hop * CORES + core).wait_send()
        for step in range(1, chips):
            sum_copy(m, step).wait_send()
        for part in range(2):
            partial_copy(m, part).wait_send()

        @pl.when(section + 1 < sections)
        def _():
            pass_copy(m).wait_send()

        return carry

    lax.fori_loop(0, micros, drain, 0)


def half_width(width):
    tiles = -(-width // LANES)
    return -(-tiles // 2) * LANES


def fits_vmem(sections, experts, micros, token_count, width, hidden):
    half = half_width(width)
    chips = experts // CORES
    block = 2 * token_count * half * 2
    held = micros * block * (experts + 3 * chips + 3) + 2 * experts * block
    held += (2 * hidden + 4 * LANES) * width * 4
    room = (width - half) % LANES + 2 * experts <= LANES and width < 2 * half
    rows_ok = token_count % 8 == 0 and chips * token_count % 16 == 0 and width % 32 == 0 and hidden % 32 == 0
    return experts % CORES == 0 and experts > CORES and room and rows_ok and held < 32 * 2**20


def whole_kernel(tokens, norm_gain, gate_up, down, routes, route_weights):
    micros, token_count, width = tokens.shape
    hidden = down.shape[2]
    sections, experts = lax.axis_size("section"), lax.axis_size("expert")
    half = half_width(width)
    chips = experts // CORES
    dims = (sections, experts, micros, token_count, width, hidden, half)
    folded_rows = 2 * token_count
    rows = experts * token_count
    dma = pltpu.SemaphoreType.DMA
    vmem = pl.BlockSpec(memory_space=pltpu.VMEM)
    hbm = pl.BlockSpec(memory_space=pl.ANY)
    work = 6 * micros * rows * width * hidden
    return pl.pallas_call(
        functools.partial(kernel, dims),
        out_shape=jax.ShapeDtypeStruct((1, micros, token_count, width), BF16),
        in_specs=[vmem, vmem, hbm, hbm, vmem, vmem],
        out_specs=vmem,
        scratch_shapes=[
            pltpu.VMEM((width, 2 * hidden), BF16),
            pltpu.VMEM((width, hidden), BF16),
            pltpu.VMEM((hidden, width), BF16),
            pltpu.VMEM((micros, folded_rows, half), BF16),
            pltpu.VMEM((micros, experts, folded_rows, half), BF16),
            pltpu.VMEM((rows, 2 * half), BF16),
            pltpu.VMEM((rows, hidden), BF16),
            pltpu.VMEM((CORES, 2, chips * token_count, half), F32),
            pltpu.VMEM((micros, 2, chips * token_count, half), BF16),
            pltpu.VMEM((micros, 2, chips * token_count, half), BF16),
            pltpu.VMEM((micros, chips, folded_rows, half), BF16),
            pltpu.VMEM((micros, chips, folded_rows, half), BF16),
            pltpu.VMEM((micros, folded_rows, half), BF16),
            pltpu.VMEM((micros, token_count, LANES), F32),
            dma((2,)),
            dma((micros, chips)),
            dma((micros, chips)),
            dma((micros, experts)),
            dma((micros, chips)),
            dma((micros, 2)),
            dma((micros, 2)),
            dma((micros, chips)),
            dma((micros, chips)),
            dma((micros,)),
            dma((micros,)),
        ],
        compiler_params=pltpu.CompilerParams(
            collective_id=0, has_side_effects=True, vmem_limit_bytes=VMEM_BYTES
        ),
        cost_estimate=pl.CostEstimate(
            flops=work, bytes_accessed=6 * width * hidden, transcendentals=micros * rows * hidden
        ),
    )(tokens, norm_gain, gate_up, down, routes.swapaxes(2, 3), route_weights.swapaxes(2, 3))


def solution(mesh):
    sections, experts = mesh.shape["section"], mesh.shape["expert"]

    def shards(tokens, norm_gain, gate_up, down, routes, route_weights):
        micros, token_count, width = tokens.shape
        hidden = down.shape[2]
        if fits_vmem(sections, experts, micros, token_count, width, hidden):
            return whole_kernel(tokens, norm_gain, gate_up, down, routes, route_weights)
        return ticked_shards(tokens, norm_gain, gate_up, down, routes, route_weights)

    return jax.shard_map(
        shards,
        mesh=mesh,
        in_specs=(
            P(None, "expert", None),
            P("section", None),
            P("section", "expert", None, None),
            P("section", "expert", None, None),
            P("section", None, "expert", None),
            P("section", None, "expert", None),
        ),
        out_specs=P("section", None, "expert", None),
        check_vma=False,
    )
```

```python
import functools

import jax
import jax.numpy as jnp
from jax import lax
from jax.experimental import pallas as pl
from jax.experimental.pallas import tpu as pltpu
from jax.sharding import PartitionSpec as P

F32 = jnp.float32
BF16 = jnp.bfloat16
LANES = 128
CORES = 2
CHUNK = 256
VMEM_BYTES = 56 * 2**20


def passed_along(value, axis, steps):
    count = lax.axis_size(axis)
    leading, last = (max(0, -steps), min(count, count - steps))
    return lax.ppermute(value, axis, [(source, source + steps) for source in range(leading, last)])


def expert_ffn(arrived, gate_up_w, down_w):
    senders, slot_count, width = arrived.shape
    hidden_units = down_w.shape[0]
    flat_rows = arrived.reshape(senders * slot_count, width)
    projected = jnp.dot(flat_rows, gate_up_w, preferred_element_type=jnp.float32)
    gate_part = projected[:, :hidden_units]
    up_part = projected[:, hidden_units:]
    activated = (gate_part * jax.nn.sigmoid(1.702 * gate_part) * (up_part + 1.0)).astype(
        jnp.bfloat16
    )
    result_rows = jnp.dot(activated, down_w, preferred_element_type=jnp.float32).astype(
        jnp.bfloat16
    )
    return result_rows.reshape(senders, slot_count, width)


def layer_step(stream, gain_row, gate_up_w, down_w, route_rows, weight_rows):
    token_count, chosen = route_rows.shape
    width = stream.shape[1]
    experts_n = lax.axis_size("expert")
    capacity = max(2, token_count * chosen * 3 // (2 * experts_n))
    widened = stream.astype(jnp.float32)
    scale = lax.rsqrt(jnp.mean(widened * widened, axis=-1, keepdims=True) + 1e-05)
    normed = (widened * scale * gain_row[None, :]).astype(jnp.bfloat16)
    flat_routes = route_rows.reshape(-1)
    matches = (flat_routes[:, None] == jnp.arange(experts_n, dtype=jnp.int32)[None, :]).astype(
        jnp.int32
    )
    slot_index = jnp.sum((jnp.cumsum(matches, axis=0) - 1) * matches, axis=1)
    target = flat_routes * capacity + slot_index
    placing = (
        jnp.arange(experts_n * capacity, dtype=jnp.int32)[:, None] == target[None, :]
    ).astype(jnp.bfloat16)
    repeated = jnp.repeat(normed, chosen, axis=0)
    outgoing = jnp.dot(placing, repeated, preferred_element_type=jnp.float32).astype(jnp.bfloat16)
    outgoing = outgoing.reshape(experts_n, capacity, width)
    arrived = lax.all_to_all(outgoing, "expert", split_axis=0, concat_axis=0, tiled=True)
    computed = expert_ffn(arrived, gate_up_w, down_w)
    returned = lax.all_to_all(computed, "expert", split_axis=0, concat_axis=0, tiled=True)
    returned_rows = returned.reshape(experts_n * capacity, width)
    gathered = jnp.take(returned_rows, target, axis=0).reshape(token_count, chosen, width)
    fixed_point = weight_rows.astype(jnp.float32)
    shares = fixed_point / jnp.sum(fixed_point, axis=-1, keepdims=True)
    accumulated = widened
    for branch in range(chosen):
        accumulated = accumulated + shares[:, branch : branch + 1] * gathered[:, branch].astype(
            jnp.float32
        )
    return accumulated.astype(jnp.bfloat16)


def ticked_shards(tokens, norm_gain, gate_up, down, routes, route_weights):
    micro_count, token_count, width = tokens.shape
    sections = lax.axis_size("section")
    section_index = lax.axis_index("section")
    gain_row = norm_gain[0]
    gate_up_w = gate_up[0, 0]
    down_w = down[0, 0]
    incoming = jnp.zeros((token_count, width), jnp.bfloat16)
    results = jnp.zeros((micro_count, token_count, width), jnp.bfloat16)
    tick_total = micro_count + sections - 1
    for tick_number in range(tick_total):
        fresh_input = tokens[min(tick_number, micro_count - 1)]
        stream = jnp.where(section_index == 0, fresh_input, incoming)
        micro_here = tick_number - section_index
        clamped = jnp.clip(micro_here, 0, micro_count - 1)
        route_rows = lax.dynamic_index_in_dim(routes[0], clamped, 0, keepdims=False)
        weight_rows = lax.dynamic_index_in_dim(route_weights[0], clamped, 0, keepdims=False)
        output_rows = layer_step(stream, gain_row, gate_up_w, down_w, route_rows, weight_rows)
        active = jnp.logical_and(micro_here >= 0, micro_here < micro_count)
        updated = lax.dynamic_update_index_in_dim(results, output_rows, clamped, 0)
        results = jnp.where(active, updated, results)
        if tick_number + 1 < tick_total:
            incoming = passed_along(output_rows, "section", 1)
    return results[None]


def folded(rows, half):
    token_count, width = rows.shape
    rest = jnp.concatenate(
        [rows[:, half:], jnp.zeros((token_count, 2 * half - width), rows.dtype)], axis=1
    )
    return jnp.concatenate([rows[:, :half], rest], axis=0)


def kernel(
    dims,
    tokens_ref, gain_ref, gate_up_hbm, down_hbm, routes_ref, weights_ref,
    out_ref,
    gate_up_w, up_w, down_w, stream, blocks, rows_x, rows_act, partial, sib_out, sib_in,
    sum_out, sum_in, passed, share_lanes,
    weight_sem, up_send, low_send, lane_recv, fwd_send, sib_send, sib_recv, sum_send, sum_recv,
    pass_send, pass_recv,
):
    sections, experts, micros, token_count, width, hidden, half = dims
    chips = experts // CORES
    second = width - half
    tile = second // LANES * LANES
    spot = second - tile
    section, me = lax.axis_index("section"), lax.axis_index("expert")
    chip, core = me // CORES, me % CORES
    sibling = chip * CORES + 1 - core

    loads = [
        pltpu.make_async_copy(gate_up_hbm.at[0, 0], gate_up_w, weight_sem.at[0]),
        pltpu.make_async_copy(down_hbm.at[0, 0], down_w, weight_sem.at[1]),
    ]
    for load in loads:
        load.start()

    def other(step):
        return lax.rem(chip + step, chips)

    def to(src, dst, send, recv, expert, sec=section):
        return pltpu.make_async_remote_copy(
            src_ref=src, dst_ref=dst, send_sem=send, recv_sem=recv,
            device_id=(sec, expert), device_id_type=pl.DeviceIdType.MESH,
        )

    barrier = pltpu.get_barrier_semaphore()
    for step in range(1, chips):
        pl.semaphore_signal(
            barrier, inc=1, device_id=(section, other(step) * CORES + core),
            device_id_type=pl.DeviceIdType.MESH,
        )
    pl.semaphore_signal(
        barrier, inc=1, device_id=(section, sibling), device_id_type=pl.DeviceIdType.MESH
    )

    @pl.when(section > 0)
    def _():
        pl.semaphore_signal(
            barrier, inc=1, device_id=(section - 1, me), device_id_type=pl.DeviceIdType.MESH
        )

    pl.semaphore_wait(barrier, chips + jnp.where(section + 1 < sections, 1, 0))

    @pl.when(section == 0)
    def _():
        for m in range(micros):
            stream[m] = folded(tokens_ref[m].astype(F32), half).astype(BF16)

    gain = folded(gain_ref[...], half)

    def up_copy(m, hop):
        owner = (chip - hop) * CORES + core
        return to(
            blocks.at[m, owner], blocks.at[m, owner], up_send.at[m, hop],
            lane_recv.at[m, owner], me + CORES,
        )

    def low_copy(m, hop):
        owner = (chip + hop) * CORES + core
        return to(
            blocks.at[m, owner], blocks.at[m, owner], low_send.at[m, hop],
            lane_recv.at[m, owner], me - CORES,
        )

    def sibling_copy(m, owner):
        return to(
            blocks.at[m, owner], blocks.at[m, owner], fwd_send.at[m, owner // CORES],
            lane_recv.at[m, owner], sibling,
        )

    def partial_copy(m, part):
        return to(
            sib_out.at[m, part], sib_in.at[m, part], sib_send.at[m, part],
            sib_recv.at[m, part], sibling,
        )

    def sum_copy(m, step):
        there = other(step)
        return to(
            sum_out.at[m, there], sum_in.at[m, chip], sum_send.at[m, step],
            sum_recv.at[m, chip], there * CORES + core,
        )

    def pass_copy(m):
        return to(
            passed.at[m], stream.at[m], pass_send.at[m], pass_recv.at[m], me,
            lax.rem(section + 1, sections),
        )

    def got_block(m, owner):
        sibling_copy(m, owner).wait_recv()

    def prepare_shares(m):
        route_rows = routes_ref[0, m]
        fixed_point = weights_ref[0, m].astype(F32)
        shares = fixed_point / jnp.sum(fixed_point, axis=0, keepdims=True)
        lane = lax.broadcasted_iota(jnp.int32, (token_count, LANES), 1) - spot
        square = (token_count, token_count)
        same = lax.broadcasted_iota(jnp.int32, square, 0) == lax.broadcasted_iota(
            jnp.int32, square, 1
        )
        first = jnp.zeros((token_count, LANES), F32)
        again = jnp.zeros((token_count, LANES), F32)
        for k in range(route_rows.shape[0]):
            named = jnp.sum(
                jnp.where(same, route_rows[k : k + 1].astype(F32), 0.0), axis=1, keepdims=True
            ).astype(jnp.int32)
            share = jnp.sum(jnp.where(same, shares[k : k + 1], 0.0), axis=1, keepdims=True)
            first = first + jnp.where(named == lane, share, 0.0)
            again = again + jnp.where(named == lane - experts, share, 0.0)
        rest = again - again.astype(BF16).astype(F32)
        share_lanes[m] = first + rest

    def send_rows(m):
        @pl.when(section > 0)
        def _():
            pass_copy(m).wait_recv()

        both = stream[m].astype(F32)
        low, high = both[:token_count], both[token_count:]
        squares = jnp.sum(low * low, axis=-1, keepdims=True) + jnp.sum(
            high * high, axis=-1, keepdims=True
        )
        scale = lax.rsqrt(squares / width + 1e-05)
        low = low * scale * gain[:1]
        high = high * scale * gain[1:]
        last = high[:, tile:] + share_lanes[m]
        high = last if tile == 0 else jnp.concatenate([high[:, :tile], last], axis=1)
        blocks[m, me] = jnp.concatenate([low, high], axis=0).astype(BF16)
        pass_block(m, 0)

    def pass_block(m, hop):
        @pl.when(jnp.logical_and(chip >= hop, chip + 1 < chips))
        def _():
            up_copy(m, hop).start()

        @pl.when(jnp.logical_and(chip + hop < chips, chip > 0))
        def _():
            low_copy(m, hop).start()

        if hop == 0:
            sibling_copy(m, me).start()

    def relay(m, hop):
        @pl.when(chip >= hop)
        def _():
            owner = (chip - hop) * CORES + core
            got_block(m, owner)

            @pl.when(chip + 1 < chips)
            def _():
                up_copy(m, hop).start()

            sibling_copy(m, owner).start()

        @pl.when(chip + hop < chips)
        def _():
            owner = (chip + hop) * CORES + core
            got_block(m, owner)

            @pl.when(chip > 0)
            def _():
                low_copy(m, hop).start()

            sibling_copy(m, owner).start()

    def project(m):
        for step in range(chips):
            got_block(m, other(step) * CORES + 1 - core)
        rows = experts * token_count
        arrived = blocks[m].astype(F32)
        low = arrived[:, :token_count].reshape(rows, half)
        high = arrived[:, token_count:].reshape(rows, half)
        lane = lax.broadcasted_iota(jnp.int32, (rows, LANES), 1) - spot
        mine = jnp.logical_or(lane == me, lane == me + experts)
        share = jnp.sum(jnp.where(mine, high[:, tile:], 0.0), axis=-1, keepdims=True)
        rows_x[:, :half] = low.astype(BF16)
        rows_x[:, half:] = high.astype(BF16)
        x = rows_x[:, :width]
        for at in range(0, hidden, CHUNK):
            upto = min(at + CHUNK, hidden)
            gate = jnp.dot(x, gate_up_w[:, at:upto], preferred_element_type=F32)
            up = jnp.dot(x, up_w[:, at:upto], preferred_element_type=F32)
            rows_act[:, at:upto] = (gate * jax.nn.sigmoid(1.702 * gate) * (up + 1.0)).astype(BF16)
        return share

    def bring_down(m, part, share):
        act = rows_act[:, :hidden]
        rows = experts * token_count
        for left in range(0, half, CHUNK):
            at = part * half + left
            room = min(CHUNK, half - left)
            upto = min(at + room, width)
            value = jnp.dot(act, down_w[:, at:upto], preferred_element_type=F32) * share
            if upto - at < room:
                value = jnp.concatenate(
                    [value, jnp.zeros((rows, room - (upto - at)), F32)], axis=1
                )
            value = value.reshape(chips, CORES, token_count, room)
            for c in range(CORES):
                partial[c, part, :, left : left + room] = value[:, c].reshape(-1, room)
        sib_out[m, part] = partial[1 - core, part].astype(BF16)
        partial_copy(m, part).start()

    def own_sum(there):
        at = pl.ds(pl.multiple_of(there * token_count, 8), token_count)
        return jnp.concatenate([partial[core, 0, at, :], partial[core, 1, at, :]], axis=0)

    def send_sums(m):
        for part in range(2):
            partial_copy(m, part).wait_recv()
            partial[core, part] = partial[core, part] + sib_in[m, part].astype(F32)
        for step in range(chips - 1, 0, -1):
            there = other(step)
            sum_out[m, there] = own_sum(there).astype(BF16)
            sum_copy(m, step).start()

    def finish(m):
        total = stream[m].astype(F32) + own_sum(chip)
        for step in range(1, chips):
            there = other(step)
            to(
                sum_out.at[m, there], sum_in.at[m, there], sum_send.at[m, step],
                sum_recv.at[m, there], there * CORES + core,
            ).wait_recv()
            total = total + sum_in[m, there].astype(F32)
        passed[m] = total.astype(BF16)

        @pl.when(section + 1 < sections)
        def _():
            pass_copy(m).start()

        out_ref[0, m] = jnp.concatenate(
            [total[:token_count], total[token_count:, :second]], axis=1
        ).astype(BF16)

    def prepare(m, carry):
        prepare_shares(m)
        return carry

    prepare_shares(0)

    @pl.when(section == 0)
    def _():
        send_rows(0)

    lax.fori_loop(1, micros, prepare, 0)
    loads[0].wait()

    def realign(i, carry):
        at = pl.ds(pl.multiple_of(i * 32, 32), 32)
        up_w[at, :] = gate_up_w[at, hidden:]
        return carry

    lax.fori_loop(0, width // 32, realign, 0)
    loads[1].wait()

    @pl.when(section > 0)
    def _():
        send_rows(0)

    for hop in range(1, chips):
        relay(0, hop)

    def step_over(m, carry):
        share = project(m)
        for part in range(2):
            bring_down(m, part, share)

        @pl.when(m + 1 < micros)
        def _():
            send_rows(m + 1)

        send_sums(m)

        @pl.when(m + 1 < micros)
        def _():
            for hop in range(1, chips):
                relay(m + 1, hop)

        finish(m)
        return carry

    lax.fori_loop(0, micros, step_over, 0)

    def drain(m, carry):
        for hop in range(chips):
            @pl.when(jnp.logical_and(chip >= hop, chip + 1 < chips))
            def _():
                up_copy(m, hop).wait_send()

            @pl.when(jnp.logical_and(chip + hop < chips, chip > 0))
            def _():
                low_copy(m, hop).wait_send()

            sibling_copy(m, hop * CORES + core).wait_send()
        for step in range(1, chips):
            sum_copy(m, step).wait_send()
        for part in range(2):
            partial_copy(m, part).wait_send()

        @pl.when(section + 1 < sections)
        def _():
            pass_copy(m).wait_send()

        return carry

    lax.fori_loop(0, micros, drain, 0)


def half_width(width):
    tiles = -(-width // LANES)
    return -(-tiles // 2) * LANES


def fits_vmem(sections, experts, micros, token_count, width, hidden):
    half = half_width(width)
    chips = experts // CORES
    block = 2 * token_count * half * 2
    held = micros * block * (experts + 3 * chips + 3) + 2 * experts * block
    held += (2 * hidden + 4 * LANES) * width * 4
    room = (width - half) % LANES + 2 * experts <= LANES and width < 2 * half
    rows_ok = token_count % 8 == 0 and chips * token_count % 16 == 0 and width % 32 == 0 and hidden % 32 == 0
    return experts % CORES == 0 and experts > CORES and room and rows_ok and held < 32 * 2**20


def whole_kernel(tokens, norm_gain, gate_up, down, routes, route_weights):
    micros, token_count, width = tokens.shape
    hidden = down.shape[2]
    sections, experts = lax.axis_size("section"), lax.axis_size("expert")
    half = half_width(width)
    chips = experts // CORES
    dims = (sections, experts, micros, token_count, width, hidden, half)
    folded_rows = 2 * token_count
    rows = experts * token_count
    dma = pltpu.SemaphoreType.DMA
    vmem = pl.BlockSpec(memory_space=pltpu.VMEM)
    hbm = pl.BlockSpec(memory_space=pl.ANY)
    work = 6 * micros * rows * width * hidden
    return pl.pallas_call(
        functools.partial(kernel, dims),
        out_shape=jax.ShapeDtypeStruct((1, micros, token_count, width), BF16),
        in_specs=[vmem, vmem, hbm, hbm, vmem, vmem],
        out_specs=vmem,
        scratch_shapes=[
            pltpu.VMEM((width, 2 * hidden), BF16),
            pltpu.VMEM((width, hidden), BF16),
            pltpu.VMEM((hidden, width), BF16),
            pltpu.VMEM((micros, folded_rows, half), BF16),
            pltpu.VMEM((micros, experts, folded_rows, half), BF16),
            pltpu.VMEM((rows, 2 * half), BF16),
            pltpu.VMEM((rows, hidden), BF16),
            pltpu.VMEM((CORES, 2, chips * token_count, half), F32),
            pltpu.VMEM((micros, 2, chips * token_count, half), BF16),
            pltpu.VMEM((micros, 2, chips * token_count, half), BF16),
            pltpu.VMEM((micros, chips, folded_rows, half), BF16),
            pltpu.VMEM((micros, chips, folded_rows, half), BF16),
            pltpu.VMEM((micros, folded_rows, half), BF16),
            pltpu.VMEM((micros, token_count, LANES), F32),
            dma((2,)),
            dma((micros, chips)),
            dma((micros, chips)),
            dma((micros, experts)),
            dma((micros, chips)),
            dma((micros, 2)),
            dma((micros, 2)),
            dma((micros, chips)),
            dma((micros, chips)),
            dma((micros,)),
            dma((micros,)),
        ],
        compiler_params=pltpu.CompilerParams(
            collective_id=0, has_side_effects=True, vmem_limit_bytes=VMEM_BYTES
        ),
        cost_estimate=pl.CostEstimate(
            flops=work, bytes_accessed=6 * width * hidden, transcendentals=micros * rows * hidden
        ),
    )(tokens, norm_gain, gate_up, down, routes.swapaxes(2, 3), route_weights.swapaxes(2, 3))


def solution(mesh):
    sections, experts = mesh.shape["section"], mesh.shape["expert"]

    def shards(tokens, norm_gain, gate_up, down, routes, route_weights):
        micros, token_count, width = tokens.shape
        hidden = down.shape[2]
        if fits_vmem(sections, experts, micros, token_count, width, hidden):
            return whole_kernel(tokens, norm_gain, gate_up, down, routes, route_weights)
        return ticked_shards(tokens, norm_gain, gate_up, down, routes, route_weights)

    return jax.shard_map(
        shards,
        mesh=mesh,
        in_specs=(
            P(None, "expert", None),
            P("section", None),
            P("section", "expert", None, None),
            P("section", "expert", None, None),
            P("section", None, "expert", None),
            P("section", None, "expert", None),
        ),
        out_specs=P("section", None, "expert", None),
        check_vma=False,
    )
```

```python
import functools

import jax
import jax.numpy as jnp
from jax import lax
from jax.experimental import pallas as pl
from jax.experimental.pallas import tpu as pltpu
from jax.sharding import PartitionSpec as P

F32 = jnp.float32
BF16 = jnp.bfloat16
LANES = 128
CORES = 2
CHUNK = 256
VMEM_BYTES = 56 * 2**20


def passed_along(value, axis, steps):
    count = lax.axis_size(axis)
    leading, last = (max(0, -steps), min(count, count - steps))
    return lax.ppermute(value, axis, [(source, source + steps) for source in range(leading, last)])


def expert_ffn(arrived, gate_up_w, down_w):
    senders, slot_count, width = arrived.shape
    hidden_units = down_w.shape[0]
    flat_rows = arrived.reshape(senders * slot_count, width)
    projected = jnp.dot(flat_rows, gate_up_w, preferred_element_type=jnp.float32)
    gate_part = projected[:, :hidden_units]
    up_part = projected[:, hidden_units:]
    activated = (gate_part * jax.nn.sigmoid(1.702 * gate_part) * (up_part + 1.0)).astype(
        jnp.bfloat16
    )
    result_rows = jnp.dot(activated, down_w, preferred_element_type=jnp.float32).astype(
        jnp.bfloat16
    )
    return result_rows.reshape(senders, slot_count, width)


def layer_step(stream, gain_row, gate_up_w, down_w, route_rows, weight_rows):
    token_count, chosen = route_rows.shape
    width = stream.shape[1]
    experts_n = lax.axis_size("expert")
    capacity = max(2, token_count * chosen * 3 // (2 * experts_n))
    widened = stream.astype(jnp.float32)
    scale = lax.rsqrt(jnp.mean(widened * widened, axis=-1, keepdims=True) + 1e-05)
    normed = (widened * scale * gain_row[None, :]).astype(jnp.bfloat16)
    flat_routes = route_rows.reshape(-1)
    matches = (flat_routes[:, None] == jnp.arange(experts_n, dtype=jnp.int32)[None, :]).astype(
        jnp.int32
    )
    slot_index = jnp.sum((jnp.cumsum(matches, axis=0) - 1) * matches, axis=1)
    target = flat_routes * capacity + slot_index
    placing = (
        jnp.arange(experts_n * capacity, dtype=jnp.int32)[:, None] == target[None, :]
    ).astype(jnp.bfloat16)
    repeated = jnp.repeat(normed, chosen, axis=0)
    outgoing = jnp.dot(placing, repeated, preferred_element_type=jnp.float32).astype(jnp.bfloat16)
    outgoing = outgoing.reshape(experts_n, capacity, width)
    arrived = lax.all_to_all(outgoing, "expert", split_axis=0, concat_axis=0, tiled=True)
    computed = expert_ffn(arrived, gate_up_w, down_w)
    returned = lax.all_to_all(computed, "expert", split_axis=0, concat_axis=0, tiled=True)
    returned_rows = returned.reshape(experts_n * capacity, width)
    gathered = jnp.take(returned_rows, target, axis=0).reshape(token_count, chosen, width)
    fixed_point = weight_rows.astype(jnp.float32)
    shares = fixed_point / jnp.sum(fixed_point, axis=-1, keepdims=True)
    accumulated = widened
    for branch in range(chosen):
        accumulated = accumulated + shares[:, branch : branch + 1] * gathered[:, branch].astype(
            jnp.float32
        )
    return accumulated.astype(jnp.bfloat16)


def ticked_shards(tokens, norm_gain, gate_up, down, routes, route_weights):
    micro_count, token_count, width = tokens.shape
    sections = lax.axis_size("section")
    section_index = lax.axis_index("section")
    gain_row = norm_gain[0]
    gate_up_w = gate_up[0, 0]
    down_w = down[0, 0]
    incoming = jnp.zeros((token_count, width), jnp.bfloat16)
    results = jnp.zeros((micro_count, token_count, width), jnp.bfloat16)
    tick_total = micro_count + sections - 1
    for tick_number in range(tick_total):
        fresh_input = tokens[min(tick_number, micro_count - 1)]
        stream = jnp.where(section_index == 0, fresh_input, incoming)
        micro_here = tick_number - section_index
        clamped = jnp.clip(micro_here, 0, micro_count - 1)
        route_rows = lax.dynamic_index_in_dim(routes[0], clamped, 0, keepdims=False)
        weight_rows = lax.dynamic_index_in_dim(route_weights[0], clamped, 0, keepdims=False)
        output_rows = layer_step(stream, gain_row, gate_up_w, down_w, route_rows, weight_rows)
        active = jnp.logical_and(micro_here >= 0, micro_here < micro_count)
        updated = lax.dynamic_update_index_in_dim(results, output_rows, clamped, 0)
        results = jnp.where(active, updated, results)
        if tick_number + 1 < tick_total:
            incoming = passed_along(output_rows, "section", 1)
    return results[None]


def folded(rows, half):
    token_count, width = rows.shape
    rest = rows[:, half:]
    if width < 2 * half:
        rest = jnp.concatenate(
            [rest, jnp.zeros((token_count, 2 * half - width), rows.dtype)], axis=1
        )
    return jnp.concatenate([rows[:, :half], rest], axis=0)


def kernel(
    dims,
    tokens_ref, gain_ref, gate_up_hbm, down_hbm, routes_ref, weights_ref,
    out_ref,
    gate_up_w, up_w, down_w, stream, blocks, rows_x, rows_act, partial, sib_out, sib_in,
    sum_out, sum_in, passed, share_lanes,
    weight_sem, lane_send, lane_recv, fwd_send, sib_send, sib_recv, sum_send, sum_recv,
    pass_send, pass_recv,
):
    sections, experts, micros, token_count, width, hidden, half = dims
    chips = experts // CORES
    second = width - half
    tile = second // LANES * LANES
    spot = second - tile
    section, me = lax.axis_index("section"), lax.axis_index("expert")
    chip, core = me // CORES, me % CORES
    sibling = chip * CORES + 1 - core

    loads = [
        pltpu.make_async_copy(gate_up_hbm.at[0, 0], gate_up_w, weight_sem.at[0]),
        pltpu.make_async_copy(down_hbm.at[0, 0], down_w, weight_sem.at[1]),
    ]
    for load in loads:
        load.start()

    def other(step):
        return lax.rem(chip + step, chips)

    def to(src, dst, send, recv, expert, sec=section):
        return pltpu.make_async_remote_copy(
            src_ref=src, dst_ref=dst, send_sem=send, recv_sem=recv,
            device_id=(sec, expert), device_id_type=pl.DeviceIdType.MESH,
        )

    barrier = pltpu.get_barrier_semaphore()
    for step in range(1, chips):
        pl.semaphore_signal(
            barrier, inc=1, device_id=(section, other(step) * CORES + core),
            device_id_type=pl.DeviceIdType.MESH,
        )
    pl.semaphore_signal(
        barrier, inc=1, device_id=(section, sibling), device_id_type=pl.DeviceIdType.MESH
    )

    @pl.when(section > 0)
    def _():
        pl.semaphore_signal(
            barrier, inc=1, device_id=(section - 1, me), device_id_type=pl.DeviceIdType.MESH
        )

    pl.semaphore_wait(barrier, chips + jnp.where(section + 1 < sections, 1, 0))

    @pl.when(section == 0)
    def _():
        for m in range(micros):
            stream[m] = folded(tokens_ref[m].astype(F32), half).astype(BF16)

    gain = folded(gain_ref[...], half)

    def lane_copy(m, step):
        return to(
            blocks.at[m, me], blocks.at[m, me], lane_send.at[m, step], lane_recv.at[m, me],
            other(step) * CORES + core,
        )

    def sibling_copy(m, owner):
        return to(
            blocks.at[m, owner], blocks.at[m, owner], fwd_send.at[m, owner // CORES],
            lane_recv.at[m, owner], sibling,
        )

    def partial_copy(m, part):
        return to(
            sib_out.at[m, part], sib_in.at[m, part], sib_send.at[m, part],
            sib_recv.at[m, part], sibling,
        )

    def sum_copy(m, part, step):
        there = other(step)
        return to(
            sum_out.at[m, part, there], sum_in.at[m, part, chip], sum_send.at[m, part, step],
            sum_recv.at[m, part, chip], there * CORES + core,
        )

    def pass_copy(m):
        return to(
            passed.at[m], stream.at[m], pass_send.at[m], pass_recv.at[m], me,
            lax.rem(section + 1, sections),
        )

    def got_block(m, owner):
        sibling_copy(m, owner).wait_recv()

    def prepare_shares(m):
        route_rows = routes_ref[0, m]
        fixed_point = weights_ref[0, m].astype(F32)
        shares = fixed_point / jnp.sum(fixed_point, axis=0, keepdims=True)
        lane = lax.broadcasted_iota(jnp.int32, (token_count, LANES), 1) - spot
        square = (token_count, token_count)
        same = lax.broadcasted_iota(jnp.int32, square, 0) == lax.broadcasted_iota(
            jnp.int32, square, 1
        )
        first = jnp.zeros((token_count, LANES), F32)
        again = jnp.zeros((token_count, LANES), F32)
        for k in range(route_rows.shape[0]):
            named = jnp.sum(
                jnp.where(same, route_rows[k : k + 1].astype(F32), 0.0), axis=1, keepdims=True
            ).astype(jnp.int32)
            share = jnp.sum(jnp.where(same, shares[k : k + 1], 0.0), axis=1, keepdims=True)
            first = first + jnp.where(named == lane, share, 0.0)
            again = again + jnp.where(named == lane - experts, share, 0.0)
        rest = again - again.astype(BF16).astype(F32)
        share_lanes[m] = first + rest

    def send_rows(m):
        @pl.when(section > 0)
        def _():
            pass_copy(m).wait_recv()

        both = stream[m].astype(F32)
        low, high = both[:token_count], both[token_count:]
        squares = jnp.sum(low * low, axis=-1, keepdims=True) + jnp.sum(
            high * high, axis=-1, keepdims=True
        )
        scale = lax.rsqrt(squares / width + 1e-05)
        low = low * scale * gain[:1]
        high = high * scale * gain[1:]
        last = high[:, tile:] + share_lanes[m]
        high = last if tile == 0 else jnp.concatenate([high[:, :tile], last], axis=1)
        blocks[m, me] = jnp.concatenate([low, high], axis=0).astype(BF16)
        for step in range(chips - 1, 0, -1):
            lane_copy(m, step).start()
        sibling_copy(m, me).start()

    def forward_rows(m):
        for step in range(1, chips):
            owner = other(step) * CORES + core
            got_block(m, owner)
            sibling_copy(m, owner).start()

    def project(m):
        for step in range(chips):
            got_block(m, other(step) * CORES + 1 - core)
        rows = experts * token_count
        arrived = blocks[m].astype(F32)
        low = arrived[:, :token_count].reshape(rows, half)
        high = arrived[:, token_count:].reshape(rows, half)
        lane = lax.broadcasted_iota(jnp.int32, (rows, LANES), 1) - spot
        mine = jnp.logical_or(lane == me, lane == me + experts)
        share = jnp.sum(jnp.where(mine, high[:, tile:], 0.0), axis=-1, keepdims=True)
        rows_x[:, :half] = low.astype(BF16)
        rows_x[:, half:] = high.astype(BF16)
        x = rows_x[:, :width]
        for at in range(0, hidden, CHUNK):
            upto = min(at + CHUNK, hidden)
            gate = jnp.dot(x, gate_up_w[:, at:upto], preferred_element_type=F32)
            up = jnp.dot(x, up_w[:, at:upto], preferred_element_type=F32)
            rows_act[:, at:upto] = (gate * jax.nn.sigmoid(1.702 * gate) * (up + 1.0)).astype(BF16)
        return share

    def bring_down(m, part, share, between):
        act = rows_act[:, :hidden]
        rows = experts * token_count
        for left in range(0, half, CHUNK):
            at = part * half + left
            room = min(CHUNK, half - left)
            if left + room == half:
                between()
            upto = min(at + room, width)
            value = jnp.dot(act, down_w[:, at:upto], preferred_element_type=F32) * share
            if upto - at < room:
                value = jnp.concatenate(
                    [value, jnp.zeros((rows, room - (upto - at)), F32)], axis=1
                )
            value = value.reshape(chips, CORES, token_count, room)
            for c in range(CORES):
                partial[c, part, :, left : left + room] = value[:, c].reshape(-1, room)
        sib_out[m, part] = partial[1 - core, part].astype(BF16)
        partial_copy(m, part).start()

    def own_sum(part, there):
        at = pl.ds(pl.multiple_of(there * token_count, 8), token_count)
        return partial[core, part, at, :]

    def send_sums(m, part):
        partial_copy(m, part).wait_recv()
        partial[core, part] = partial[core, part] + sib_in[m, part].astype(F32)
        for step in range(chips - 1, 0, -1):
            there = other(step)
            sum_out[m, part, there] = folded(own_sum(part, there), half // 2).astype(BF16)
            sum_copy(m, part, step).start()

    def finish(m):
        total = stream[m].astype(F32)
        sums = []
        for part in range(2):
            quarters = jnp.zeros((2 * token_count, half // 2), F32)
            for step in range(1, chips):
                there = other(step)
                to(
                    sum_out.at[m, part, there], sum_in.at[m, part, there],
                    sum_send.at[m, part, step], sum_recv.at[m, part, there],
                    there * CORES + core,
                ).wait_recv()
                quarters = quarters + sum_in[m, part, there].astype(F32)
            sums.append(
                own_sum(part, chip)
                + jnp.concatenate([quarters[:token_count], quarters[token_count:]], axis=1)
            )
        total = total + jnp.concatenate(sums, axis=0)
        passed[m] = total.astype(BF16)

        @pl.when(section + 1 < sections)
        def _():
            pass_copy(m).start()

        out_ref[0, m] = jnp.concatenate(
            [total[:token_count], total[token_count:, :second]], axis=1
        ).astype(BF16)

    def prepare(m, carry):
        prepare_shares(m)
        return carry

    prepare_shares(0)

    @pl.when(section == 0)
    def _():
        send_rows(0)

    lax.fori_loop(1, micros, prepare, 0)
    loads[0].wait()

    def realign(i, carry):
        at = pl.ds(pl.multiple_of(i * 32, 32), 32)
        up_w[at, :] = gate_up_w[at, hidden:]
        return carry

    lax.fori_loop(0, width // 32, realign, 0)
    loads[1].wait()

    @pl.when(section > 0)
    def _():
        send_rows(0)

    forward_rows(0)

    def step_over(m, carry):
        share = project(m)
        bring_down(m, 0, share, lambda: None)
        bring_down(m, 1, share, lambda: send_sums(m, 0))
        send_sums(m, 1)

        @pl.when(m + 1 < micros)
        def _():
            send_rows(m + 1)

        finish(m)

        @pl.when(m + 1 < micros)
        def _():
            forward_rows(m + 1)

        return carry

    lax.fori_loop(0, micros, step_over, 0)

    def drain(m, carry):
        for step in range(chips):
            sibling_copy(m, step * CORES + core).wait_send()
        for step in range(1, chips):
            lane_copy(m, step).wait_send()
            for part in range(2):
                sum_copy(m, part, step).wait_send()
        for part in range(2):
            partial_copy(m, part).wait_send()

        @pl.when(section + 1 < sections)
        def _():
            pass_copy(m).wait_send()

        return carry

    lax.fori_loop(0, micros, drain, 0)


def half_width(width):
    tiles = -(-width // LANES)
    return -(-tiles // 2) * LANES


def fits_vmem(sections, experts, micros, token_count, width, hidden):
    half = half_width(width)
    chips = experts // CORES
    if half % (2 * LANES):
        return False
    block = 2 * token_count * half * 2
    held = micros * block * (experts + 3 * chips + 3) + 2 * experts * block
    held += (2 * hidden + 4 * LANES) * width * 4
    room = (width - half) % LANES + 2 * experts <= LANES and width < 2 * half
    rows_ok = token_count % 8 == 0 and chips * token_count % 16 == 0 and width % 32 == 0 and hidden % 32 == 0
    return experts % CORES == 0 and experts > CORES and room and rows_ok and held < 32 * 2**20


def whole_kernel(tokens, norm_gain, gate_up, down, routes, route_weights):
    micros, token_count, width = tokens.shape
    hidden = down.shape[2]
    sections, experts = lax.axis_size("section"), lax.axis_size("expert")
    half = half_width(width)
    chips = experts // CORES
    dims = (sections, experts, micros, token_count, width, hidden, half)
    folded_rows = 2 * token_count
    rows = experts * token_count
    dma = pltpu.SemaphoreType.DMA
    vmem = pl.BlockSpec(memory_space=pltpu.VMEM)
    hbm = pl.BlockSpec(memory_space=pl.ANY)
    work = 6 * micros * rows * width * hidden
    return pl.pallas_call(
        functools.partial(kernel, dims),
        out_shape=jax.ShapeDtypeStruct((1, micros, token_count, width), BF16),
        in_specs=[vmem, vmem, hbm, hbm, vmem, vmem],
        out_specs=vmem,
        scratch_shapes=[
            pltpu.VMEM((width, 2 * hidden), BF16),
            pltpu.VMEM((width, hidden), BF16),
            pltpu.VMEM((hidden, width), BF16),
            pltpu.VMEM((micros, folded_rows, half), BF16),
            pltpu.VMEM((micros, experts, folded_rows, half), BF16),
            pltpu.VMEM((rows, 2 * half), BF16),
            pltpu.VMEM((rows, hidden), BF16),
            pltpu.VMEM((CORES, 2, chips * token_count, half), F32),
            pltpu.VMEM((micros, 2, chips * token_count, half), BF16),
            pltpu.VMEM((micros, 2, chips * token_count, half), BF16),
            pltpu.VMEM((micros, 2, chips, folded_rows, half // 2), BF16),
            pltpu.VMEM((micros, 2, chips, folded_rows, half // 2), BF16),
            pltpu.VMEM((micros, folded_rows, half), BF16),
            pltpu.VMEM((micros, token_count, LANES), F32),
            dma((2,)),
            dma((micros, chips)),
            dma((micros, experts)),
            dma((micros, chips)),
            dma((micros, 2)),
            dma((micros, 2)),
            dma((micros, 2, chips)),
            dma((micros, 2, chips)),
            dma((micros,)),
            dma((micros,)),
        ],
        compiler_params=pltpu.CompilerParams(
            collective_id=0, has_side_effects=True, vmem_limit_bytes=VMEM_BYTES
        ),
        cost_estimate=pl.CostEstimate(
            flops=work, bytes_accessed=6 * width * hidden, transcendentals=micros * rows * hidden
        ),
    )(tokens, norm_gain, gate_up, down, routes.swapaxes(2, 3), route_weights.swapaxes(2, 3))


def solution(mesh):
    sections, experts = mesh.shape["section"], mesh.shape["expert"]

    def shards(tokens, norm_gain, gate_up, down, routes, route_weights):
        micros, token_count, width = tokens.shape
        hidden = down.shape[2]
        if fits_vmem(sections, experts, micros, token_count, width, hidden):
            return whole_kernel(tokens, norm_gain, gate_up, down, routes, route_weights)
        return ticked_shards(tokens, norm_gain, gate_up, down, routes, route_weights)

    return jax.shard_map(
        shards,
        mesh=mesh,
        in_specs=(
            P(None, "expert", None),
            P("section", None),
            P("section", "expert", None, None),
            P("section", "expert", None, None),
            P("section", None, "expert", None),
            P("section", None, "expert", None),
        ),
        out_specs=P("section", None, "expert", None),
        check_vma=False,
    )
```
